32 devices in a mesh: parts: 2 (over y), context: 16 (over z, x, core).
Axes of the slice: x: 2, y: 2, z: 4, core: 2. Of those that a mesh axis runs over, the one named last changes fastest.
Arguments:
- projected: bfloat16 [4096, 12288], P(('parts', 'context')), parts along dimension 0, may hold values from -6 to 6
- short_taps: float32 [3, 12288], replicated, may hold values from -3.5 to 3.5
- residues: float32 [4096, 16], replicated, may hold values from -1.5 to 1.5
- rates: float32 [4096, 16], replicated, may hold values from 9.765625e-06 to 0.05
- skip: float32 [4096], replicated, may hold values from 0.5 to 1.5
Outputs:
- gated: bfloat16 [4096, 4096], P(('parts', 'context')), parts along dimension 0
The draws below stay inside these ranges and needn't reach their ends.
There are 2 independent parts, one for each index of `parts`. The reference program is written for one: setup_inputs(seed, part) draws one part's arguments, and reference() takes and returns one part's arrays. A program takes and returns all parts, laid end to end along the dimension named above; an argument that names none is the same for every part. Nothing has to cross between parts.
All inputs are finite; a program needn't handle non-finite values.
Results may differ from the reference program's by a relative error of at most 0.0057.
Values may be sent and summed in bfloat16 or wider, within the bound.
A program may use at most 128 MiB of HBM per device.

```python
import math
import jax
import jax.numpy as jnp
from jax import lax

CH = 4096
MODES = 16
SHORT = 3
TOKENS = 2048


def block_scale(own_key, extent, cuts, smallest, largest):
    def one(dim, shards_of):
        steps = jax.random.uniform(jax.random.fold_in(jax.random.fold_in(own_key, 6), dim), (shards_of,), jnp.float32, smallest / len(cuts), largest / len(cuts))
        return jnp.repeat(jnp.exp(steps), extent[dim] // shards_of).reshape((-1,) + (1,) * (len(extent) - dim - 1))

    loudness = one(*cuts[0])
    for cut in cuts[1:]:
        loudness = loudness * one(*cut)
    return loudness


def scatter_about(stream_key, dims, scale, reach, pieces=(), dtype=jnp.bfloat16):
    values = scale * jax.random.normal(stream_key, dims, jnp.float32)
    if pieces:
        values = values * block_scale(stream_key, dims, pieces, -0.22, 0.18)
    return jnp.clip(values, -reach, reach).astype(dtype)


def setup_inputs(seed: int = 0, part: int = 0) -> dict:
    seeds = jax.random.split(jax.random.key(seed), 6)
    own_keys = jax.random.split(jax.random.fold_in(seeds[5], part), 6)
    projected = scatter_about(own_keys[0], (TOKENS, 3 * CH), 1.0, 6.0, ((0, 16),))
    short_taps = scatter_about(seeds[1], (SHORT, 3 * CH), SHORT ** -0.5, 3.5, (), jnp.float32)
    residues = scatter_about(seeds[2], (CH, MODES), MODES ** -0.5, 1.5, (), jnp.float32)
    rates = jnp.clip(jnp.exp(jax.random.uniform(seeds[3], (CH, MODES), jnp.float32, math.log(9.765624781721272e-06), math.log(0.05))), 9.765624781721272e-06, 0.05)
    skip = jnp.clip(jax.random.uniform(seeds[4], (CH,), jnp.float32, 0.5, 1.5), 0.5, 1.5)
    return {"projected": projected, "short_taps": short_taps, "residues": residues, "rates": rates, "skip": skip}


def short_filter(projected, short_taps):
    width = projected.shape[1]
    padded = jnp.concatenate([jnp.zeros((SHORT - 1, width), jnp.float32), projected.astype(jnp.float32)], axis=0)
    length = projected.shape[0]
    result = jnp.zeros((length, width), jnp.float32)
    for step in range(SHORT):
        result = result + short_taps[step][None, :] * padded[SHORT - 1 - step:SHORT - 1 - step + length]
    return result

def reference(projected, short_taps, residues, rates, skip):
    pre = short_filter(projected, short_taps)
    first = pre[:, :CH]
    stream = (pre[:, CH:2 * CH] * pre[:, 2 * CH:]).astype(jnp.bfloat16)
    coef = residues * jnp.sqrt(-jnp.expm1(-2.0 * rates))
    length = TOKENS
    lags = jnp.arange(length).astype(jnp.float32)
    block = math.gcd(CH, 256)
    count = CH // block
    stream_t = stream.astype(jnp.float32).T.reshape(count, block, length)
    coef_b = coef.reshape(count, block, MODES)
    rate_b = rates.reshape(count, block, MODES)

    def one_block(args):
        signal, factor, decay = args
        filt = jnp.zeros((block, length), jnp.float32)
        for mode in range(MODES):
            filt = filt + factor[:, mode][:, None] * jnp.exp(-decay[:, mode][:, None] * lags[None, :])
        spectrum = jnp.fft.rfft(signal, n=2 * length, axis=-1) * jnp.fft.rfft(filt, n=2 * length, axis=-1)
        return jnp.fft.irfft(spectrum, n=2 * length, axis=-1)[:, :length]
    conv = lax.map(one_block, (stream_t, coef_b, rate_b)).reshape(CH, length).T
    mixed = (conv + skip[None, :] * stream.astype(jnp.float32)).astype(jnp.bfloat16)
    return (first * mixed.astype(jnp.float32)).astype(jnp.bfloat16)
```

```python
import functools

import jax
import jax.numpy as jnp
from jax import lax
from jax.experimental import pallas as pl
from jax.experimental.pallas import tpu as pltpu
from jax.sharding import PartitionSpec as P

SHORT = 3
LANES = 128
SUB = 8
TILE = SUB * LANES
MESH = pl.DeviceIdType.MESH
F32 = jnp.float32
BF16 = jnp.bfloat16


def one_less_exp(x):
    series = x * (
        1.0
        - x * (1 / 2) * (1.0 - x * (1 / 3) * (1.0 - x * (1 / 4) * (1.0 - x * (1 / 5) * (1.0 - x * (1 / 6)))))
    )
    return jnp.where(x < 0.125, series, 1.0 - jnp.exp(-x))


def tree_sum(values):
    values = list(values)
    while len(values) > 1:
        paired = [values[k] + values[k + 1] for k in range(0, len(values) - 1, 2)]
        if len(values) % 2:
            paired.append(values[-1])
        values = paired
    return values[0]


def kernel(
    n, rows, groups, modes,
    proj, taps, res, rate, skip, out,
    pin, rim, rim_f, rim_out, rim_in, px, z, y, pout, av, cv, dkv, tv,
    sent, got, back, carry,
    in_sems, rim_sem, out_sems, halo_send, halo_recv, send1, recv1, send2, recv2,
):
    me = lax.axis_index("context")
    tiles = groups // SUB
    share = modes * groups // n

    barrier = pltpu.get_barrier_semaphore()

    def greet(k, c):
        pl.semaphore_signal(
            barrier, inc=1, device_id={"context": lax.rem(me + k, n)}, device_id_type=MESH
        )
        return c

    lax.fori_loop(1, n, greet, 0)

    rim_copy = pltpu.make_async_copy(proj.at[pl.ds(rows - 16, 16), :], rim, rim_sem)
    rim_copy.start()

    def tile_copy(i):
        return pltpu.make_async_copy(
            proj.at[:, pl.ds(pl.multiple_of(i * TILE, TILE), TILE)], pin.at[i], in_sems.at[i]
        )

    def start_in(i, c):
        tile_copy(i).start()
        return c

    lax.fori_loop(0, 3 * tiles, start_in, 0)

    rim_copy.wait()

    def cut_rim(i, c):
        for j in range(SUB):
            cols = rim[:, pl.ds(pl.multiple_of(i * TILE + j * LANES, LANES), LANES)].astype(F32)
            rim_f[pl.ds(i * 16 + j, 2, stride=SUB), :] = cols[14:16]
        return c

    lax.fori_loop(0, 3 * tiles, cut_rim, 0)
    rim_out[...] = rim_f[...].astype(BF16)
    pl.semaphore_wait(barrier, n - 1)
    halo = pltpu.make_async_remote_copy(
        src_ref=rim_out,
        dst_ref=rim_in,
        send_sem=halo_send,
        recv_sem=halo_recv,
        device_id={"context": lax.rem(me + 1, n)},
        device_id_type=MESH,
    )

    @pl.when(me < n - 1)
    def _():
        halo.start()

    def params(j, c):
        cols = pl.ds(pl.multiple_of(j * LANES, LANES), LANES)
        r = rate[:, cols]
        where = pl.ds(j, modes, stride=groups)
        av[where, :] = jnp.exp(-r)
        dkv[where, :] = jnp.exp(-float(rows) * r)
        cv[where, :] = res[:, cols] * jnp.sqrt(one_less_exp(2.0 * r))
        return c

    lax.fori_loop(0, groups, params, 0)

    def set_taps(j, c):
        cols = pl.ds(pl.multiple_of(j * LANES, LANES), LANES)
        tv[pl.ds(j, SHORT, stride=3 * groups), :] = taps[:, cols]
        return c

    lax.fori_loop(0, 3 * groups, set_taps, 0)

    def spread(i, c):
        tile_copy(i).wait()
        for j in range(SUB):
            px[i, pl.ds(2 * SUB + j, rows, stride=SUB), :] = pin[
                i, :, j * LANES : (j + 1) * LANES
            ].astype(F32)
        return c

    lax.fori_loop(0, 3 * tiles, spread, 0)

    @pl.when(me < n - 1)
    def _():
        halo.wait_send()

    @pl.when(me > 0)
    def _():
        halo.wait_recv()

    @pl.when(me == 0)
    def _():
        rim_in[...] = jnp.zeros_like(rim_in)

    for i in range(3 * tiles):
        px[i, 0 : 2 * SUB, :] = rim_in[i * 16 : i * 16 + 16, :].astype(F32)

    def part(ref, m, i):
        return ref[pl.ds(pl.multiple_of(m * groups + i * SUB, SUB), SUB), :]

    def taps_of(stream, i):
        return [part(tv, 3 * k + stream, i) for k in range(SHORT)]

    def pre(tap, stream, i, t):
        total = None
        for k in range(SHORT):
            row = pl.multiple_of((t + SHORT - 1 - k) * SUB, SUB)
            term = tap[k] * px[stream * tiles + i, pl.ds(row, SUB), :]
            total = term if total is None else total + term
        return total

    def at(t):
        return pl.ds(pl.multiple_of(t * SUB, SUB), SUB)

    def put_state(ref, m, i, value):
        if share >= SUB:
            per = groups // share
            ref[m * per + (i * SUB) // share, pl.ds(pl.multiple_of((i * SUB) % share, SUB), SUB), :] = value
        else:
            count = SUB // share
            for k in range(count):
                ref[(m * groups + i * SUB) // share + k] = value[k * share : (k + 1) * share]

    def get_state(ref, m, i):
        if share >= SUB:
            per = groups // share
            return ref[m * per + (i * SUB) // share, pl.ds(pl.multiple_of((i * SUB) % share, SUB), SUB), :]
        count = SUB // share
        return jnp.concatenate(
            [ref[(m * groups + i * SUB) // share + k] for k in range(count)], axis=0
        )

    zeros = tuple(jnp.zeros((SUB, LANES), F32) for _ in range(modes))

    def end_states(i, c):
        a = [part(av, m, i) for m in range(modes)]
        tap2, tap3 = taps_of(1, i), taps_of(2, i)

        def step(t, h):
            zt = (pre(tap2, 1, i, t) * pre(tap3, 2, i, t)).astype(BF16).astype(F32)
            z[i, at(t), :] = zt
            return tuple(a[m] * h[m] + zt for m in range(modes))

        h = lax.fori_loop(0, rows, step, zeros, unroll=4)
        for m in range(modes):
            put_state(sent, m, i, h[m])
        return c

    lax.fori_loop(0, tiles, end_states, 0)

    def exchange(src, dst, send_sem, recv_sem):
        def one(k, c):
            other = lax.rem(me + k, n)
            pltpu.make_async_remote_copy(
                src_ref=src.at[other],
                dst_ref=dst.at[me],
                send_sem=send_sem,
                recv_sem=recv_sem,
                device_id={"context": other},
                device_id_type=MESH,
            ).start()
            return c

        lax.fori_loop(1, n, one, 0)
        dst[me] = src[me]

    def finish(src, dst, send_sem, recv_sem):
        most = pl.ds(0, n - 1)
        pltpu.make_async_copy(src.at[most], src.at[most], send_sem).wait()
        pltpu.make_async_copy(dst.at[most], dst.at[most], recv_sem).wait()

    exchange(sent, got, send1, recv1)

    def local(i, c):
        a = [part(av, m, i) for m in range(modes)]
        coef = [part(cv, m, i) for m in range(modes)]
        direct = part(skip, 0, i)

        def step(t, h):
            zt = z[i, at(t), :]
            h = tuple(a[m] * h[m] + zt for m in range(modes))
            y[i, at(t), :] = direct * zt + tree_sum(coef[m] * h[m] for m in range(modes))
            return h

        lax.fori_loop(0, rows, step, zeros, unroll=4)
        return c

    lax.fori_loop(0, tiles // 2, local, 0)
    finish(sent, got, send1, recv1)

    decay = dkv[pl.ds(me * share, share), :]

    def scan(d, held):
        back[d] = held
        return decay * held + got[d]

    lax.fori_loop(0, n, scan, jnp.zeros((share, LANES), F32))
    exchange(back, carry, send2, recv2)
    lax.fori_loop(tiles // 2, tiles, local, 0)
    finish(back, carry, send2, recv2)

    def out_copy(i):
        return pltpu.make_async_copy(
            pout.at[i], out.at[:, pl.ds(pl.multiple_of(i * TILE, TILE), TILE)], out_sems.at[i]
        )

    def close(i, c):
        a = [part(av, m, i) for m in range(modes)]
        tap1 = taps_of(0, i)
        g = tuple(part(cv, m, i) * get_state(carry, m, i) for m in range(modes))

        def step(t, g):
            g = tuple(a[m] * g[m] for m in range(modes))
            mixed = (y[i, at(t), :] + tree_sum(g)).astype(BF16).astype(F32)
            y[i, at(t), :] = pre(tap1, 0, i, t) * mixed
            return g

        lax.fori_loop(0, rows, step, g, unroll=4)
        for j in range(SUB):
            pout[i, :, j * LANES : (j + 1) * LANES] = y[
                i, pl.ds(j, rows, stride=SUB), :
            ].astype(BF16)
        out_copy(i).start()
        return c

    lax.fori_loop(0, tiles, close, 0)

    def end_out(i, c):
        out_copy(i).wait()
        return c

    lax.fori_loop(0, tiles, end_out, 0)


def per_device(projected, short_taps, residues, rates, skip):
    n = lax.axis_size("context")
    rows, width = projected.shape
    channels = width // 3
    modes = residues.shape[1]
    groups = channels // LANES
    tiles = channels // TILE
    share = modes * groups // n
    vmem = pl.BlockSpec(memory_space=pltpu.VMEM)
    hbm = pl.BlockSpec(memory_space=pl.ANY)
    dma = pltpu.SemaphoreType.DMA
    states = pltpu.VMEM((n, share, LANES), F32)
    flat = pltpu.VMEM((modes * groups, LANES), F32)
    return pl.pallas_call(
        functools.partial(kernel, n, rows, groups, modes),
        out_shape=jax.ShapeDtypeStruct((rows, channels), BF16),
        in_specs=[hbm, vmem, vmem, vmem, vmem],
        out_specs=hbm,
        scratch_shapes=[
            pltpu.VMEM((3 * tiles, rows, TILE), BF16),
            pltpu.VMEM((16, width), BF16),
            pltpu.VMEM((3 * tiles * 16, LANES), F32),
            pltpu.VMEM((3 * tiles * 16, LANES), BF16),
            pltpu.VMEM((3 * tiles * 16, LANES), BF16),
            pltpu.VMEM((3 * tiles, (rows + 2) * SUB, LANES), F32),
            pltpu.VMEM((tiles, rows * SUB, LANES), F32),
            pltpu.VMEM((tiles, rows * SUB, LANES), F32),
            pltpu.VMEM((tiles, rows, TILE), BF16),
            flat,
            flat,
            flat,
            pltpu.VMEM((SHORT * 3 * groups, LANES), F32),
            states,
            states,
            states,
            states,
            dma((3 * tiles,)),
            dma,
            dma((tiles,)),
            dma,
            dma,
            dma,
            dma,
            dma,
            dma,
        ],
        compiler_params=pltpu.CompilerParams(
            collective_id=0, has_side_effects=True, vmem_limit_bytes=48 * 1024 * 1024
        ),
        cost_estimate=pl.CostEstimate(
            flops=rows * channels * modes * 8, bytes_accessed=rows * channels * 8, transcendentals=0
        ),
    )(projected, short_taps, residues.T, rates.T, skip.reshape(groups, LANES))


def solution(mesh):
    in_specs = (P(("parts", "context"), None), P(), P(), P(), P())
    out_specs = P(("parts", "context"), None)
    return jax.shard_map(
        per_device, mesh=mesh, in_specs=in_specs, out_specs=out_specs, check_vma=False
    )
```

```python
import functools

import jax
import jax.numpy as jnp
from jax import lax
from jax.experimental import pallas as pl
from jax.experimental.pallas import tpu as pltpu
from jax.sharding import PartitionSpec as P

SHORT = 3
LANES = 128
SUB = 8
TILE = SUB * LANES
MESH = pl.DeviceIdType.MESH
F32 = jnp.float32
BF16 = jnp.bfloat16
WIRE = BF16
UNROLL = 7


def one_less_exp(x):
    series = x * (
        1.0
        - x * (1 / 2) * (1.0 - x * (1 / 3) * (1.0 - x * (1 / 4) * (1.0 - x * (1 / 5) * (1.0 - x * (1 / 6)))))
    )
    return jnp.where(x < 0.125, series, 1.0 - jnp.exp(-x))


def tree_sum(values):
    values = list(values)
    while len(values) > 1:
        paired = [values[k] + values[k + 1] for k in range(0, len(values) - 1, 2)]
        if len(values) % 2:
            paired.append(values[-1])
        values = paired
    return values[0]


def kernel(
    n, rows, groups, modes, owners,
    proj, taps_hbm, res_hbm, rate_hbm, skip_hbm, out,
    taps, res, rate, skip, small_sems,
    pin, rim_out, rim_in, px, z, y, first, pout, av, cv, tv,
    sent_f, sent, got, back, carry, carry_f,
    in_sems, out_sems, halo_send, halo_recv, send1, recv1, send2, recv2,
):
    me = lax.axis_index("context")
    tiles = groups // SUB
    per = groups // owners
    height = modes + 8

    barrier = pltpu.get_barrier_semaphore()

    def greet(k, c):
        pl.semaphore_signal(
            barrier, inc=1, device_id={"context": lax.rem(me + k, n)}, device_id_type=MESH
        )
        return c

    lax.fori_loop(1, n, greet, 0)

    small = [
        pltpu.make_async_copy(src, dst, small_sems.at[k])
        for k, (src, dst) in enumerate(
            [(rate_hbm, rate), (res_hbm, res), (taps_hbm, taps), (skip_hbm, skip)]
        )
    ]
    for copy in small:
        copy.start()

    def tile_copy(i):
        return pltpu.make_async_copy(
            proj.at[:, pl.ds(pl.multiple_of(i * TILE, TILE), TILE)], pin.at[i], in_sems.at[i]
        )

    def start_in(i, c):
        tile_copy(i).start()
        return c

    lax.fori_loop(tiles, 3 * tiles, start_in, 0)
    lax.fori_loop(0, tiles, start_in, 0)
    for copy in small:
        copy.wait()

    def params(j, c):
        cols = pl.ds(pl.multiple_of(j * LANES, LANES), LANES)
        r = rate[:, cols]
        where = pl.ds(j, modes, stride=groups)
        av[where, :] = jnp.exp(-r)
        cv[where, :] = res[:, cols] * jnp.sqrt(one_less_exp(2.0 * r))
        return c

    lax.fori_loop(0, groups, params, 0, unroll=4)

    def set_taps(j, c):
        cols = pl.ds(pl.multiple_of(j * LANES, LANES), LANES)
        tv[pl.ds(j, SHORT, stride=3 * groups), :] = taps[:, cols]
        return c

    lax.fori_loop(0, 3 * groups, set_taps, 0, unroll=8)

    def spread(i, c):
        tile_copy(i).wait()
        for j in range(SUB):
            px[i, pl.ds(2 * SUB + j, rows, stride=SUB), :] = pin[
                i, :, j * LANES : (j + 1) * LANES
            ].astype(F32)
        return c

    lax.fori_loop(tiles, 3 * tiles, spread, 0)

    def part(ref, m, i):
        return ref[pl.ds(pl.multiple_of(m * groups + i * SUB, SUB), SUB), :]

    def taps_of(stream, i):
        return [part(tv, 3 * k + stream, i) for k in range(SHORT)]

    def at(t):
        return pl.ds(pl.multiple_of(t * SUB, SUB), SUB)

    def token(stream, i, t):
        return px[stream * tiles + i, at(t + SHORT - 1), :]

    def pre(tap, stream, i, t):
        total = None
        for k in range(SHORT):
            term = tap[k] * token(stream, i, t - k)
            total = term if total is None else total + term
        return total

    def rounded(value):
        return value.astype(BF16).astype(F32)

    zeros = tuple(jnp.zeros((SUB, LANES), F32) for _ in range(modes))

    def end_states(i, c):
        a = [part(av, m, i) for m in range(modes)]
        tap2, tap3 = taps_of(1, i), taps_of(2, i)

        def step(t, h):
            zt = rounded(pre(tap2, 1, i, t) * pre(tap3, 2, i, t))
            z[i, at(t), :] = zt
            return tuple(a[m] * h[m] + zt for m in range(modes))

        h = lax.fori_loop(SHORT - 1, rows, step, zeros, unroll=UNROLL)
        edges = [token(s, i, t) for t in (0, 1, rows - 2, rows - 1) for s in (1, 2)]
        for m, value in enumerate(list(h) + edges):
            sent_f[pl.ds(i * SUB * height + m, SUB, stride=height), :] = value
        return c

    lax.fori_loop(0, tiles, end_states, 0)
    own = per * height
    for j in range(owners):
        sent[j, 0:own, :] = sent_f[j * own : (j + 1) * own, :].astype(WIRE)

    lax.fori_loop(0, tiles, spread, 0)
    for i in range(3 * tiles):
        rim_out[i * 16 : i * 16 + 16, :] = px[i, rows * SUB : (rows + 2) * SUB, :].astype(BF16)

    pl.semaphore_wait(barrier, n - 1)

    def send(src, dst, other, send_sem, recv_sem):
        pltpu.make_async_remote_copy(
            src_ref=src.at[other],
            dst_ref=dst.at[me],
            send_sem=send_sem,
            recv_sem=recv_sem,
            device_id={"context": other},
            device_id_type=MESH,
        ).start()

    def spend(ref, count, sem):
        most = pl.ds(0, count)
        pltpu.make_async_copy(ref.at[most], ref.at[most], sem).wait()

    def for_owner(body):
        if owners == n:
            body()
        else:
            pl.when(me < owners)(body)

    def for_other(body):
        if owners < n:
            pl.when(me >= owners)(body)

    def send_states(k, c):
        send(sent, got, lax.rem(me + k, owners), send1, recv1)
        return c

    @for_owner
    def _():
        lax.fori_loop(1, owners, send_states, 0)
        got[me] = sent[me]

    @for_other
    def _():
        lax.fori_loop(0, owners, send_states, 0)

    halo = pltpu.make_async_remote_copy(
        src_ref=rim_out,
        dst_ref=rim_in,
        send_sem=halo_send,
        recv_sem=halo_recv,
        device_id={"context": lax.rem(me + 1, n)},
        device_id_type=MESH,
    )

    @pl.when(me < n - 1)
    def _():
        halo.start()

    def local(i, c):
        a = [part(av, m, i) for m in range(modes)]
        coef = [part(cv, m, i) for m in range(modes)]
        direct = part(skip, 0, i)
        tap1 = taps_of(0, i)

        def step(t, h):
            zt = z[i, at(t), :]
            h = tuple(a[m] * h[m] + zt for m in range(modes))
            y[i, at(t), :] = direct * zt + tree_sum(coef[m] * h[m] for m in range(modes))
            first[i, at(t), :] = pre(tap1, 0, i, t)
            return h

        lax.fori_loop(SHORT - 1, rows, step, zeros, unroll=UNROLL)
        return c

    lax.fori_loop(0, tiles // 2, local, 0)

    @for_owner
    def _():
        spend(got, n - 1, recv1)
        decay, step1, late, tap2, tap3 = [], [], [], [], []
        for q in range(per):
            group = me * per + q
            r = rate[:, pl.ds(pl.multiple_of(group * LANES, LANES), LANES)]
            decay.append(jnp.exp(-float(rows) * r))
            late.append(jnp.exp(-float(rows - 2) * r))
            step1.append(jnp.exp(-r))
            for tap, stream in ((tap2, 1), (tap3, 2)):
                tap.append(
                    [tv[pl.ds((3 * k + stream) * groups + group, 1), :] for k in range(SHORT)]
                )

        def scan(d, held):
            block = got[d].astype(F32)
            following, returned = [], []
            for q in range(per):
                state, last = held[q]
                base = q * height
                edge = [block[base + modes + k : base + modes + k + 1] for k in range(8)]
                x0, v0, x1, v1 = edge[:4]
                xb, vb, xa, va = last

                def three(tap, now, before, ahead):
                    return tap[0] * now + tap[1] * before + tap[2] * ahead

                z0 = rounded(three(tap2[q], x0, xa, xb) * three(tap3[q], v0, va, vb))
                z1 = rounded(three(tap2[q], x1, x0, xa) * three(tap3[q], v1, v0, va))
                returned.append(state)
                state = (
                    decay[q] * state
                    + block[base : base + modes]
                    + late[q] * (step1[q] * z0 + z1)
                )
                following.append((state, tuple(edge[4:])))
            back[d] = jnp.concatenate(returned, axis=0).astype(WIRE)
            return tuple(following)

        none = tuple(jnp.zeros((1, LANES), F32) for _ in range(4))
        start = tuple((jnp.zeros((modes, LANES), F32), none) for _ in range(per))
        lax.fori_loop(0, n, scan, start, unroll=4)

        def send_back(k, c):
            send(back, carry, lax.rem(me + k, n), send2, recv2)
            return c

        lax.fori_loop(1, n, send_back, 0)
        carry[me] = back[me]

    lax.fori_loop(tiles // 2, tiles, local, 0)

    @pl.when(me < n - 1)
    def _():
        halo.wait_send()

    @pl.when(me > 0)
    def _():
        halo.wait_recv()

    @pl.when(me == 0)
    def _():
        rim_in[...] = jnp.zeros_like(rim_in)

    for i in range(3 * tiles):
        px[i, 0 : 2 * SUB, :] = rim_in[i * 16 : i * 16 + 16, :].astype(F32)

    @for_owner
    def _():
        spend(sent, owners - 1, send1)
        spend(back, n - 1, send2)
        spend(carry, owners - 1, recv2)

    @for_other
    def _():
        spend(sent, owners, send1)
        spend(carry, owners, recv2)

    for j in range(owners):
        carry_f[j * per * modes : (j + 1) * per * modes, :] = carry[j].astype(F32)

    def out_copy(i):
        return pltpu.make_async_copy(
            pout.at[i], out.at[:, pl.ds(pl.multiple_of(i * TILE, TILE), TILE)], out_sems.at[i]
        )

    def close(i, c):
        a = [part(av, m, i) for m in range(modes)]
        coef = [part(cv, m, i) for m in range(modes)]
        direct = part(skip, 0, i)
        tap1, tap2, tap3 = [taps_of(stream, i) for stream in range(3)]
        h = [carry_f[pl.ds(i * SUB * modes + m, SUB, stride=modes), :] for m in range(modes)]
        for t in range(SHORT - 1):
            zt = rounded(pre(tap2, 1, i, t) * pre(tap3, 2, i, t))
            h = [a[m] * h[m] + zt for m in range(modes)]
            mixed = rounded(direct * zt + tree_sum(coef[m] * h[m] for m in range(modes)))
            z[i, at(t), :] = pre(tap1, 0, i, t) * mixed
        g = tuple(coef[m] * h[m] for m in range(modes))

        def step(t, g):
            g = tuple(a[m] * g[m] for m in range(modes))
            mixed = rounded(y[i, at(t), :] + tree_sum(g))
            z[i, at(t), :] = first[i, at(t), :] * mixed
            return g

        lax.fori_loop(SHORT - 1, rows, step, g, unroll=UNROLL)
        for j in range(SUB):
            pout[i, :, j * LANES : (j + 1) * LANES] = z[
                i, pl.ds(j, rows, stride=SUB), :
            ].astype(BF16)
        out_copy(i).start()
        return c

    lax.fori_loop(0, tiles, close, 0)

    def end_out(i, c):
        out_copy(i).wait()
        return c

    lax.fori_loop(0, tiles, end_out, 0)


def per_device(projected, short_taps, residues, rates, skip):
    n = lax.axis_size("context")
    rows, width = projected.shape
    channels = width // 3
    modes = residues.shape[1]
    groups = channels // LANES
    tiles = channels // TILE
    owners = min(n, groups)
    per = groups // owners
    height = modes + 8
    padded = -(-per * height // 16) * 16
    hbm = pl.BlockSpec(memory_space=pl.ANY)
    dma = pltpu.SemaphoreType.DMA
    flat = pltpu.VMEM((modes * groups, LANES), F32)
    tokens = pltpu.VMEM((tiles, rows * SUB, LANES), F32)
    rims = pltpu.VMEM((3 * tiles * 16, LANES), BF16)
    return pl.pallas_call(
        functools.partial(kernel, n, rows, groups, modes, owners),
        out_shape=jax.ShapeDtypeStruct((rows, channels), BF16),
        in_specs=[hbm] * 5,
        out_specs=hbm,
        scratch_shapes=[
            pltpu.VMEM((SHORT, width), F32),
            pltpu.VMEM((modes, channels), F32),
            pltpu.VMEM((modes, channels), F32),
            pltpu.VMEM((groups, LANES), F32),
            dma((4,)),
            pltpu.VMEM((3 * tiles, rows, TILE), BF16),
            rims,
            rims,
            pltpu.VMEM((3 * tiles, (rows + 2) * SUB, LANES), F32),
            tokens,
            tokens,
            tokens,
            pltpu.VMEM((tiles, rows, TILE), BF16),
            flat,
            flat,
            pltpu.VMEM((SHORT * 3 * groups, LANES), F32),
            pltpu.VMEM((groups * height, LANES), F32),
            pltpu.VMEM((owners, padded, LANES), WIRE),
            pltpu.VMEM((n, padded, LANES), WIRE),
            pltpu.VMEM((n, per * modes, LANES), WIRE),
            pltpu.VMEM((owners, per * modes, LANES), WIRE),
            flat,
            dma((3 * tiles,)),
            dma((tiles,)),
            dma,
            dma,
            dma,
            dma,
            dma,
            dma,
        ],
        compiler_params=pltpu.CompilerParams(
            collective_id=0, has_side_effects=True, vmem_limit_bytes=60 * 1024 * 1024
        ),
        cost_estimate=pl.CostEstimate(
            flops=rows * channels * modes * 8, bytes_accessed=rows * channels * 8, transcendentals=0
        ),
    )(projected, short_taps, residues.T, rates.T, skip.reshape(groups, LANES))


def solution(mesh):
    in_specs = (P(("parts", "context"), None), P(), P(), P(), P())
    out_specs = P(("parts", "context"), None)
    return jax.shard_map(
        per_device, mesh=mesh, in_specs=in_specs, out_specs=out_specs, check_vma=False
    )
```

```python
import functools

import jax
import jax.numpy as jnp
from jax import lax
from jax.experimental import pallas as pl
from jax.experimental.pallas import tpu as pltpu
from jax.sharding import PartitionSpec as P

SHORT = 3
LANES = 128
SUB = 8
TILE = SUB * LANES
MESH = pl.DeviceIdType.MESH
F32 = jnp.float32
BF16 = jnp.bfloat16
WIRE = BF16
UNROLL = 7


def one_less_exp(x):
    series = x * (
        1.0
        - x * (1 / 2) * (1.0 - x * (1 / 3) * (1.0 - x * (1 / 4) * (1.0 - x * (1 / 5) * (1.0 - x * (1 / 6)))))
    )
    return jnp.where(x < 0.125, series, 1.0 - jnp.exp(-x))


def tree_sum(values):
    values = list(values)
    while len(values) > 1:
        paired = [values[k] + values[k + 1] for k in range(0, len(values) - 1, 2)]
        if len(values) % 2:
            paired.append(values[-1])
        values = paired
    return values[0]


def kernel(
    n, rows, groups, modes, owners,
    proj, taps_hbm, res_hbm, rate_hbm, skip_hbm, out,
    taps, res, rate, skip, small_sems,
    pin, rim_out, rim_in, px, z, y, first, av, cv, tv,
    sent_f, sent, got, back, carry, carry_f,
    in_sems, halo_send, halo_recv, send1, recv1, send2, recv2,
):
    me = lax.axis_index("context")
    tiles = groups // SUB
    per = groups // owners
    height = modes + 8
    own = per * height
    crew = SUB // per
    home = lax.rem(me, owners) // crew

    def turn(k):
        return lax.rem(home + k, tiles)

    barrier = pltpu.get_barrier_semaphore()

    def greet(k, c):
        pl.semaphore_signal(
            barrier, inc=1, device_id={"context": lax.rem(me + k, n)}, device_id_type=MESH
        )
        return c

    lax.fori_loop(1, n, greet, 0)

    small = [
        pltpu.make_async_copy(src, dst, small_sems.at[k])
        for k, (src, dst) in enumerate(
            [(rate_hbm, rate), (taps_hbm, taps), (res_hbm, res), (skip_hbm, skip)]
        )
    ]
    small[0].start()
    small[1].start()

    def tile_copy(i):
        return pltpu.make_async_copy(
            proj.at[:, pl.ds(pl.multiple_of(i * TILE, TILE), TILE)], pin.at[i], in_sems.at[i]
        )

    def start_in(i, c):
        tile_copy(i).start()
        return c

    for k in range(1, tiles + 1):
        tile_copy(tiles + turn(k)).start()
        tile_copy(2 * tiles + turn(k)).start()
    lax.fori_loop(0, tiles, start_in, 0)
    small[2].start()
    small[3].start()
    small[0].wait()
    small[1].wait()

    def params(j, c):
        cols = pl.ds(pl.multiple_of(j * LANES, LANES), LANES)
        av[pl.ds(j, modes, stride=groups), :] = jnp.exp(-rate[:, cols])
        return c

    lax.fori_loop(0, groups, params, 0, unroll=4)

    def set_taps(j, c):
        cols = pl.ds(pl.multiple_of(j * LANES, LANES), LANES)
        tv[pl.ds(j, SHORT, stride=3 * groups), :] = taps[:, cols]
        return c

    lax.fori_loop(0, 3 * groups, set_taps, 0, unroll=8)

    def spread(i, c):
        tile_copy(i).wait()
        for j in range(SUB):
            px[i, pl.ds(2 * SUB + j, rows, stride=SUB), :] = pin[
                i, :, j * LANES : (j + 1) * LANES
            ].astype(F32)
        return c


    def part(ref, m, i):
        return ref[pl.ds(pl.multiple_of(m * groups + i * SUB, SUB), SUB), :]

    def taps_of(stream, i):
        return [part(tv, 3 * k + stream, i) for k in range(SHORT)]

    def at(t):
        return pl.ds(pl.multiple_of(t * SUB, SUB), SUB)

    def token(stream, i, t):
        return px[stream * tiles + i, at(t + SHORT - 1), :]

    def pre(tap, stream, i, t):
        total = None
        for k in range(SHORT):
            term = tap[k] * token(stream, i, t - k)
            total = term if total is None else total + term
        return total

    def rounded(value):
        return value.astype(BF16).astype(F32)

    zeros = tuple(jnp.zeros((SUB, LANES), F32) for _ in range(modes))

    def end_states(i):
        spread(tiles + i, 0)
        spread(2 * tiles + i, 0)
        a = [part(av, m, i) for m in range(modes)]
        tap2, tap3 = taps_of(1, i), taps_of(2, i)

        def step(t, h):
            zt = rounded(pre(tap2, 1, i, t) * pre(tap3, 2, i, t))
            z[i, at(t), :] = zt
            return tuple(a[m] * h[m] + zt for m in range(modes))

        h = lax.fori_loop(SHORT - 1, rows, step, zeros, unroll=UNROLL)
        edges = [token(s, i, t) for t in (0, 1, rows - 2, rows - 1) for s in (1, 2)]
        for m, value in enumerate(list(h) + edges):
            sent_f[pl.ds(i * SUB * height + m, SUB, stride=height), :] = value
        for k in range(crew):
            j = i * crew + k
            sent[j, 0:own, :] = sent_f[pl.ds(pl.multiple_of(j * own, SUB), own), :].astype(WIRE)

    def send(src, dst, other, send_sem, recv_sem):
        pltpu.make_async_remote_copy(
            src_ref=src.at[other],
            dst_ref=dst.at[me],
            send_sem=send_sem,
            recv_sem=recv_sem,
            device_id={"context": other},
            device_id_type=MESH,
        ).start()

    def spend(ref, count, sem):
        most = pl.ds(0, count)
        pltpu.make_async_copy(ref.at[most], ref.at[most], sem).wait()

    def for_owner(body):
        if owners == n:
            body()
        else:
            pl.when(me < owners)(body)

    def for_other(body):
        if owners < n:
            pl.when(me >= owners)(body)

    def ship(i):
        for k in range(crew):
            j = i * crew + k

            @pl.when(j != me)
            def _():
                send(sent, got, j, send1, recv1)

    def pass_tile(k, c):
        end_states(turn(k))
        ship(turn(k))
        return c

    end_states(turn(1))
    pl.semaphore_wait(barrier, n - 1)
    ship(turn(1))
    lax.fori_loop(2, tiles + 1, pass_tile, 0)

    @for_owner
    def _():
        got[me] = sent[me]

    lax.fori_loop(0, tiles, spread, 0)
    for i in range(3 * tiles):
        rim_out[i * 16 : i * 16 + 16, :] = px[i, rows * SUB : (rows + 2) * SUB, :].astype(BF16)

    halo = pltpu.make_async_remote_copy(
        src_ref=rim_out,
        dst_ref=rim_in,
        send_sem=halo_send,
        recv_sem=halo_recv,
        device_id={"context": lax.rem(me + 1, n)},
        device_id_type=MESH,
    )

    @pl.when(me < n - 1)
    def _():
        halo.start()

    small[2].wait()
    small[3].wait()

    def coefs(j, c):
        cols = pl.ds(pl.multiple_of(j * LANES, LANES), LANES)
        cv[pl.ds(j, modes, stride=groups), :] = res[:, cols] * jnp.sqrt(
            one_less_exp(2.0 * rate[:, cols])
        )
        return c

    lax.fori_loop(0, groups, coefs, 0, unroll=4)

    def local(i, c):
        a = [part(av, m, i) for m in range(modes)]
        coef = [part(cv, m, i) for m in range(modes)]
        direct = part(skip, 0, i)
        tap1 = taps_of(0, i)

        def step(t, h):
            zt = z[i, at(t), :]
            h = tuple(a[m] * h[m] + zt for m in range(modes))
            y[i, at(t), :] = direct * zt + tree_sum(coef[m] * h[m] for m in range(modes))
            first[i, at(t), :] = pre(tap1, 0, i, t)
            return h

        lax.fori_loop(SHORT - 1, rows, step, zeros, unroll=UNROLL)
        return c

    lax.fori_loop(0, tiles // 2, local, 0)

    @for_owner
    def _():
        spend(got, n - 1, recv1)
        decay, step1, late, tap2, tap3 = [], [], [], [], []
        for q in range(per):
            group = me * per + q
            r = rate[:, pl.ds(pl.multiple_of(group * LANES, LANES), LANES)]
            decay.append(jnp.exp(-float(rows) * r))
            late.append(jnp.exp(-float(rows - 2) * r))
            step1.append(jnp.exp(-r))
            for tap, stream in ((tap2, 1), (tap3, 2)):
                tap.append(
                    [tv[pl.ds((3 * k + stream) * groups + group, 1), :] for k in range(SHORT)]
                )

        def scan(d, held):
            block = got[d].astype(F32)
            following, returned = [], []
            for q in range(per):
                state, last = held[q]
                base = q * height
                edge = [block[base + modes + k : base + modes + k + 1] for k in range(8)]
                x0, v0, x1, v1 = edge[:4]
                xb, vb, xa, va = last

                def three(tap, now, before, ahead):
                    return tap[0] * now + tap[1] * before + tap[2] * ahead

                z0 = rounded(three(tap2[q], x0, xa, xb) * three(tap3[q], v0, va, vb))
                z1 = rounded(three(tap2[q], x1, x0, xa) * three(tap3[q], v1, v0, va))
                returned.append(state)
                state = (
                    decay[q] * state
                    + block[base : base + modes]
                    + late[q] * (step1[q] * z0 + z1)
                )
                following.append((state, tuple(edge[4:])))
            back[d] = jnp.concatenate(returned, axis=0).astype(WIRE)
            return tuple(following)

        none = tuple(jnp.zeros((1, LANES), F32) for _ in range(4))
        start = tuple((jnp.zeros((modes, LANES), F32), none) for _ in range(per))
        lax.fori_loop(0, n, scan, start, unroll=4)

        def send_back(k, c):
            send(back, carry, lax.rem(me + k, n), send2, recv2.at[home])
            return c

        lax.fori_loop(1, n, send_back, 0)
        carry[me] = back[me]

    lax.fori_loop(tiles // 2, tiles, local, 0)

    @pl.when(me < n - 1)
    def _():
        halo.wait_send()

    @pl.when(me > 0)
    def _():
        halo.wait_recv()

    @pl.when(me == 0)
    def _():
        rim_in[...] = jnp.zeros_like(rim_in)

    for i in range(3 * tiles):
        px[i, 0 : 2 * SUB, :] = rim_in[i * 16 : i * 16 + 16, :].astype(F32)

    def close(k, c):
        i = turn(k)

        @pl.when(jnp.logical_and(k == 0, me < owners))
        def _():
            spend(carry, crew - 1, recv2.at[i])

        @pl.when(jnp.logical_or(k > 0, me >= owners))
        def _():
            spend(carry, crew, recv2.at[i])

        for j in range(crew):
            chunk = per * modes
            carry_f[pl.ds(pl.multiple_of((i * crew + j) * chunk, SUB), chunk), :] = carry[
                i * crew + j
            ].astype(F32)
        a = [part(av, m, i) for m in range(modes)]
        coef = [part(cv, m, i) for m in range(modes)]
        direct = part(skip, 0, i)
        tap1, tap2, tap3 = [taps_of(stream, i) for stream in range(3)]
        h = [carry_f[pl.ds(i * SUB * modes + m, SUB, stride=modes), :] for m in range(modes)]
        for t in range(SHORT - 1):
            zt = rounded(pre(tap2, 1, i, t) * pre(tap3, 2, i, t))
            h = [a[m] * h[m] + zt for m in range(modes)]
            mixed = rounded(direct * zt + tree_sum(coef[m] * h[m] for m in range(modes)))
            z[i, at(t), :] = pre(tap1, 0, i, t) * mixed
        g = tuple(coef[m] * h[m] for m in range(modes))

        def step(t, g):
            g = tuple(a[m] * g[m] for m in range(modes))
            mixed = rounded(y[i, at(t), :] + tree_sum(g))
            z[i, at(t), :] = first[i, at(t), :] * mixed
            return g

        lax.fori_loop(SHORT - 1, rows, step, g, unroll=UNROLL)
        for j in range(SUB):
            cols = pl.ds(pl.multiple_of(i * TILE + j * LANES, LANES), LANES)
            out[:, cols] = z[
                i, pl.ds(j, rows, stride=SUB), :
            ].astype(BF16)
        return c

    lax.fori_loop(0, tiles, close, 0)

    @for_owner
    def _():
        spend(sent, owners - 1, send1)
        spend(back, n - 1, send2)

    @for_other
    def _():
        spend(sent, owners, send1)


def per_device(projected, short_taps, residues, rates, skip):
    n = lax.axis_size("context")
    rows, width = projected.shape
    channels = width // 3
    modes = residues.shape[1]
    groups = channels // LANES
    tiles = channels // TILE
    owners = min(n, groups)
    per = groups // owners
    height = modes + 8
    padded = -(-per * height // 16) * 16
    hbm = pl.BlockSpec(memory_space=pl.ANY)
    dma = pltpu.SemaphoreType.DMA
    flat = pltpu.VMEM((modes * groups, LANES), F32)
    tokens = pltpu.VMEM((tiles, rows * SUB, LANES), F32)
    rims = pltpu.VMEM((3 * tiles * 16, LANES), BF16)
    return pl.pallas_call(
        functools.partial(kernel, n, rows, groups, modes, owners),
        out_shape=pltpu.VMEM((rows, channels), BF16),
        in_specs=[hbm] * 5,
        out_specs=pl.BlockSpec(memory_space=pltpu.VMEM),
        scratch_shapes=[
            pltpu.VMEM((SHORT, width), F32),
            pltpu.VMEM((modes, channels), F32),
            pltpu.VMEM((modes, channels), F32),
            pltpu.VMEM((groups, LANES), F32),
            dma((4,)),
            pltpu.VMEM((3 * tiles, rows, TILE), BF16),
            rims,
            rims,
            pltpu.VMEM((3 * tiles, (rows + 2) * SUB, LANES), F32),
            tokens,
            tokens,
            tokens,
            flat,
            flat,
            pltpu.VMEM((SHORT * 3 * groups, LANES), F32),
            pltpu.VMEM((groups * height, LANES), F32),
            pltpu.VMEM((owners, padded, LANES), WIRE),
            pltpu.VMEM((n, padded, LANES), WIRE),
            pltpu.VMEM((n, per * modes, LANES), WIRE),
            pltpu.VMEM((owners, per * modes, LANES), WIRE),
            flat,
            dma((3 * tiles,)),
            dma,
            dma,
            dma,
            dma,
            dma,
            dma((tiles,)),
        ],
        compiler_params=pltpu.CompilerParams(
            collective_id=0, has_side_effects=True, vmem_limit_bytes=60 * 1024 * 1024
        ),
        cost_estimate=pl.CostEstimate(
            flops=rows * channels * modes * 8, bytes_accessed=rows * channels * 8, transcendentals=0
        ),
    )(projected, short_taps, residues.T, rates.T, skip.reshape(groups, LANES))


def solution(mesh):
    in_specs = (P(("parts", "context"), None), P(), P(), P(), P())
    out_specs = P(("parts", "context"), None)
    return jax.shard_map(
        per_device, mesh=mesh, in_specs=in_specs, out_specs=out_specs, check_vma=False
    )
```

```python
import functools

import jax
import jax.numpy as jnp
from jax import lax
from jax.experimental import pallas as pl
from jax.experimental.pallas import tpu as pltpu
from jax.sharding import PartitionSpec as P

SHORT = 3
LANES = 128
SUB = 8
TILE = SUB * LANES
MESH = pl.DeviceIdType.MESH
F32 = jnp.float32
BF16 = jnp.bfloat16
WIRE = BF16
UNROLL = 14


def one_less_exp(x):
    series = x * (
        1.0
        - x * (1 / 2) * (1.0 - x * (1 / 3) * (1.0 - x * (1 / 4) * (1.0 - x * (1 / 5) * (1.0 - x * (1 / 6)))))
    )
    return jnp.where(x < 0.125, series, 1.0 - jnp.exp(-x))


def tree_sum(values):
    values = list(values)
    while len(values) > 1:
        paired = [values[k] + values[k + 1] for k in range(0, len(values) - 1, 2)]
        if len(values) % 2:
            paired.append(values[-1])
        values = paired
    return values[0]


def kernel(
    n, rows, groups, modes, owners,
    proj, taps_hbm, res_hbm, rate_hbm, skip_hbm, out,
    taps, res, rate, skip, small_sems,
    pin, rim_out, rim_in, px, z, y, first, av, cv, tv,
    sent_f, sent, got, back, carry, carry_f,
    in_sems, halo_send, halo_recv, send1, recv1, send2, recv2,
):
    me = lax.axis_index("context")
    tiles = groups // SUB
    per = groups // owners
    height = modes + 8
    own = per * height
    crew = SUB // per
    home = lax.rem(me, owners) // crew

    def turn(k):
        return lax.rem(home + k, tiles)

    barrier = pltpu.get_barrier_semaphore()

    def greet(k, c):
        pl.semaphore_signal(
            barrier, inc=1, device_id={"context": lax.rem(me + k, n)}, device_id_type=MESH
        )
        return c

    lax.fori_loop(1, n, greet, 0)

    small = [
        pltpu.make_async_copy(src, dst, small_sems.at[k])
        for k, (src, dst) in enumerate(
            [(rate_hbm, rate), (taps_hbm, taps), (res_hbm, res), (skip_hbm, skip)]
        )
    ]
    small[0].start()
    small[1].start()

    def tile_copy(i):
        return pltpu.make_async_copy(
            proj.at[:, pl.ds(pl.multiple_of(i * TILE, TILE), TILE)], pin.at[i], in_sems.at[i]
        )

    def start_in(i, c):
        tile_copy(i).start()
        return c

    for k in range(1, tiles + 1):
        tile_copy(tiles + turn(k)).start()
        tile_copy(2 * tiles + turn(k)).start()
    lax.fori_loop(0, tiles, start_in, 0)
    small[2].start()
    small[3].start()
    small[0].wait()
    small[1].wait()

    def params(j, c):
        cols = pl.ds(pl.multiple_of(j * LANES, LANES), LANES)
        av[pl.ds(j, modes, stride=groups), :] = jnp.exp(-rate[:, cols])
        return c

    lax.fori_loop(0, groups, params, 0, unroll=4)

    def set_taps(j, c):
        cols = pl.ds(pl.multiple_of(j * LANES, LANES), LANES)
        tv[pl.ds(j, SHORT, stride=3 * groups), :] = taps[:, cols]
        return c

    lax.fori_loop(groups, 3 * groups, set_taps, 0, unroll=8)

    def spread(i, c):
        tile_copy(i).wait()
        for j in range(SUB):
            px[i, pl.ds(2 * SUB + j, rows, stride=SUB), :] = pin[
                i, :, j * LANES : (j + 1) * LANES
            ].astype(F32)
        return c


    def part(ref, m, i):
        return ref[pl.ds(pl.multiple_of(m * groups + i * SUB, SUB), SUB), :]

    def taps_of(stream, i):
        return [part(tv, 3 * k + stream, i) for k in range(SHORT)]

    def at(t):
        return pl.ds(pl.multiple_of(t * SUB, SUB), SUB)

    def token(stream, i, t):
        return px[stream * tiles + i, at(t + SHORT - 1), :]

    def pre(tap, stream, i, t):
        total = None
        for k in range(SHORT):
            term = tap[k] * token(stream, i, t - k)
            total = term if total is None else total + term
        return total

    def rounded(value):
        return value.astype(BF16).astype(F32)

    zeros = tuple(jnp.zeros((SUB, LANES), F32) for _ in range(modes))

    def end_states(i):
        spread(tiles + i, 0)
        spread(2 * tiles + i, 0)
        a = [part(av, m, i) for m in range(modes)]
        tap2, tap3 = taps_of(1, i), taps_of(2, i)

        def step(t, h):
            zt = rounded(pre(tap2, 1, i, t) * pre(tap3, 2, i, t))
            z[i, at(t), :] = zt
            return tuple(a[m] * h[m] + zt for m in range(modes))

        h = lax.fori_loop(SHORT - 1, rows, step, zeros, unroll=UNROLL)
        edges = [token(s, i, t) for t in (0, 1, rows - 2, rows - 1) for s in (1, 2)]
        for m, value in enumerate(list(h) + edges):
            sent_f[pl.ds(i * SUB * height + m, SUB, stride=height), :] = value
        for k in range(crew):
            j = i * crew + k
            sent[j, 0:own, :] = sent_f[pl.ds(pl.multiple_of(j * own, SUB), own), :].astype(WIRE)

    def send(src, dst, other, send_sem, recv_sem):
        pltpu.make_async_remote_copy(
            src_ref=src.at[other],
            dst_ref=dst.at[me],
            send_sem=send_sem,
            recv_sem=recv_sem,
            device_id={"context": other},
            device_id_type=MESH,
        ).start()

    def spend(ref, count, sem):
        most = pl.ds(0, count)
        pltpu.make_async_copy(ref.at[most], ref.at[most], sem).wait()

    def for_owner(body):
        if owners == n:
            body()
        else:
            pl.when(me < owners)(body)

    def for_other(body):
        if owners < n:
            pl.when(me >= owners)(body)

    def ship(i):
        for k in range(crew):
            j = i * crew + k

            @pl.when(j != me)
            def _():
                send(sent, got, j, send1, recv1)

    def pass_tile(k, c):
        end_states(turn(k))
        ship(turn(k))
        return c

    end_states(turn(1))
    pl.semaphore_wait(barrier, n - 1)
    ship(turn(1))
    lax.fori_loop(2, tiles + 1, pass_tile, 0)

    @for_owner
    def _():
        got[me] = sent[me]

    lax.fori_loop(0, tiles, spread, 0)
    for i in range(3 * tiles):
        rim_out[i * 16 : i * 16 + 16, :] = px[i, rows * SUB : (rows + 2) * SUB, :].astype(BF16)

    halo = pltpu.make_async_remote_copy(
        src_ref=rim_out,
        dst_ref=rim_in,
        send_sem=halo_send,
        recv_sem=halo_recv,
        device_id={"context": lax.rem(me + 1, n)},
        device_id_type=MESH,
    )

    @pl.when(me < n - 1)
    def _():
        halo.start()

    small[2].wait()
    small[3].wait()

    def coefs(j, c):
        cols = pl.ds(pl.multiple_of(j * LANES, LANES), LANES)
        cv[pl.ds(j, modes, stride=groups), :] = res[:, cols] * jnp.sqrt(
            one_less_exp(2.0 * rate[:, cols])
        )
        return c

    lax.fori_loop(0, groups, coefs, 0, unroll=4)
    lax.fori_loop(0, groups, set_taps, 0, unroll=8)

    def local(i, c):
        a = [part(av, m, i) for m in range(modes)]
        coef = [part(cv, m, i) for m in range(modes)]
        direct = part(skip, 0, i)
        tap1 = taps_of(0, i)

        def step(t, h):
            zt = z[i, at(t), :]
            h = tuple(a[m] * h[m] + zt for m in range(modes))
            y[i, at(t), :] = direct * zt + tree_sum(coef[m] * h[m] for m in range(modes))
            first[i, at(t), :] = pre(tap1, 0, i, t)
            return h

        lax.fori_loop(SHORT - 1, rows, step, zeros, unroll=UNROLL)
        return c

    lax.fori_loop(0, tiles // 2, local, 0)

    @for_owner
    def _():
        spend(got, n - 1, recv1)
        decay, step1, late, tap2, tap3 = [], [], [], [], []
        for q in range(per):
            group = me * per + q
            r = rate[:, pl.ds(pl.multiple_of(group * LANES, LANES), LANES)]
            decay.append(jnp.exp(-float(rows) * r))
            late.append(jnp.exp(-float(rows - 2) * r))
            step1.append(jnp.exp(-r))
            for tap, stream in ((tap2, 1), (tap3, 2)):
                tap.append(
                    [tv[pl.ds((3 * k + stream) * groups + group, 1), :] for k in range(SHORT)]
                )

        def scan(d, held):
            block = got[d].astype(F32)
            following, returned = [], []
            for q in range(per):
                state, last = held[q]
                base = q * height
                edge = [block[base + modes + k : base + modes + k + 1] for k in range(8)]
                x0, v0, x1, v1 = edge[:4]
                xb, vb, xa, va = last

                def three(tap, now, before, ahead):
                    return tap[0] * now + tap[1] * before + tap[2] * ahead

                z0 = rounded(three(tap2[q], x0, xa, xb) * three(tap3[q], v0, va, vb))
                z1 = rounded(three(tap2[q], x1, x0, xa) * three(tap3[q], v1, v0, va))
                returned.append(state)
                state = (
                    decay[q] * state
                    + block[base : base + modes]
                    + late[q] * (step1[q] * z0 + z1)
                )
                following.append((state, tuple(edge[4:])))
            back[d] = jnp.concatenate(returned, axis=0).astype(WIRE)
            return tuple(following)

        none = tuple(jnp.zeros((1, LANES), F32) for _ in range(4))
        start = tuple((jnp.zeros((modes, LANES), F32), none) for _ in range(per))
        lax.fori_loop(0, n, scan, start, unroll=4)

        def send_back(k, c):
            send(back, carry, lax.rem(me + k, n), send2, recv2.at[home])
            return c

        lax.fori_loop(1, n, send_back, 0)
        carry[me] = back[me]

    lax.fori_loop(tiles // 2, tiles, local, 0)

    @pl.when(me < n - 1)
    def _():
        halo.wait_send()

    @pl.when(me > 0)
    def _():
        halo.wait_recv()

    @pl.when(me == 0)
    def _():
        rim_in[...] = jnp.zeros_like(rim_in)

    for i in range(3 * tiles):
        px[i, 0 : 2 * SUB, :] = rim_in[i * 16 : i * 16 + 16, :].astype(F32)

    def close(k, c):
        i = turn(k)

        @pl.when(jnp.logical_and(k == 0, me < owners))
        def _():
            spend(carry, crew - 1, recv2.at[i])

        @pl.when(jnp.logical_or(k > 0, me >= owners))
        def _():
            spend(carry, crew, recv2.at[i])

        for j in range(crew):
            chunk = per * modes
            carry_f[pl.ds(pl.multiple_of((i * crew + j) * chunk, SUB), chunk), :] = carry[
                i * crew + j
            ].astype(F32)
        a = [part(av, m, i) for m in range(modes)]
        coef = [part(cv, m, i) for m in range(modes)]
        direct = part(skip, 0, i)
        tap1, tap2, tap3 = [taps_of(stream, i) for stream in range(3)]
        h = [carry_f[pl.ds(i * SUB * modes + m, SUB, stride=modes), :] for m in range(modes)]
        for t in range(SHORT - 1):
            zt = rounded(pre(tap2, 1, i, t) * pre(tap3, 2, i, t))
            h = [a[m] * h[m] + zt for m in range(modes)]
            mixed = rounded(direct * zt + tree_sum(coef[m] * h[m] for m in range(modes)))
            z[i, at(t), :] = pre(tap1, 0, i, t) * mixed
        g = tuple(coef[m] * h[m] for m in range(modes))

        def step(t, g):
            g = tuple(a[m] * g[m] for m in range(modes))
            mixed = rounded(y[i, at(t), :] + tree_sum(g))
            z[i, at(t), :] = first[i, at(t), :] * mixed
            return g

        lax.fori_loop(SHORT - 1, rows, step, g, unroll=UNROLL)
        for j in range(SUB):
            cols = pl.ds(pl.multiple_of(i * TILE + j * LANES, LANES), LANES)
            out[:, cols] = z[
                i, pl.ds(j, rows, stride=SUB), :
            ].astype(BF16)
        return c

    lax.fori_loop(0, tiles, close, 0)

    @for_owner
    def _():
        spend(sent, owners - 1, send1)
        spend(back, n - 1, send2)

    @for_other
    def _():
        spend(sent, owners, send1)


def per_device(projected, short_taps, residues, rates, skip):
    n = lax.axis_size("context")
    rows, width = projected.shape
    channels = width // 3
    modes = residues.shape[1]
    groups = channels // LANES
    tiles = channels // TILE
    owners = min(n, groups)
    per = groups // owners
    height = modes + 8
    padded = -(-per * height // 16) * 16
    hbm = pl.BlockSpec(memory_space=pl.ANY)
    dma = pltpu.SemaphoreType.DMA
    flat = pltpu.VMEM((modes * groups, LANES), F32)
    tokens = pltpu.VMEM((tiles, rows * SUB, LANES), F32)
    rims = pltpu.VMEM((3 * tiles * 16, LANES), BF16)
    return pl.pallas_call(
        functools.partial(kernel, n, rows, groups, modes, owners),
        out_shape=pltpu.VMEM((rows, channels), BF16),
        in_specs=[hbm] * 5,
        out_specs=pl.BlockSpec(memory_space=pltpu.VMEM),
        scratch_shapes=[
            pltpu.VMEM((SHORT, width), F32),
            pltpu.VMEM((modes, channels), F32),
            pltpu.VMEM((modes, channels), F32),
            pltpu.VMEM((groups, LANES), F32),
            dma((4,)),
            pltpu.VMEM((3 * tiles, rows, TILE), BF16),
            rims,
            rims,
            pltpu.VMEM((3 * tiles, (rows + 2) * SUB, LANES), F32),
            tokens,
            tokens,
            tokens,
            flat,
            flat,
            pltpu.VMEM((SHORT * 3 * groups, LANES), F32),
            pltpu.VMEM((groups * height, LANES), F32),
            pltpu.VMEM((owners, padded, LANES), WIRE),
            pltpu.VMEM((n, padded, LANES), WIRE),
            pltpu.VMEM((n, per * modes, LANES), WIRE),
            pltpu.VMEM((owners, per * modes, LANES), WIRE),
            flat,
            dma((3 * tiles,)),
            dma,
            dma,
            dma,
            dma,
            dma,
            dma((tiles,)),
        ],
        compiler_params=pltpu.CompilerParams(
            collective_id=0, has_side_effects=True, vmem_limit_bytes=60 * 1024 * 1024
        ),
        cost_estimate=pl.CostEstimate(
            flops=rows * channels * modes * 8, bytes_accessed=rows * channels * 8, transcendentals=0
        ),
    )(projected, short_taps, residues.T, rates.T, skip.reshape(groups, LANES))


def solution(mesh):
    in_specs = (P(("parts", "context"), None), P(), P(), P(), P())
    out_specs = P(("parts", "context"), None)
    return jax.shard_map(
        per_device, mesh=mesh, in_specs=in_specs, out_specs=out_specs, check_vma=False
    )
```
